32 devices in a mesh: section: 2 (over y), ident: 16 (over z, x, core).
Axes of the slice: x: 2, y: 2, z: 4, core: 2. Of those that a mesh axis runs over, the one named last changes fastest.
Arguments:
- inputs: bfloat16 [16, 192, 1024], P('ident'), may hold values from -6 to 6
- section_weight: bfloat16 [2, 1024, 1024], P('section'), may hold values from -0.1875 to 0.1875
- section_gain: float32 [2, 1024], P('section'), may hold values from 0.25 to 1.75
- neck_weight: bfloat16 [1024, 512], replicated, may hold values from -0.1875 to 0.1875
- centers: bfloat16 [16, 2, 3, 128, 512], P('ident'), may hold values from -6 to 6
- sampled: int32 [16, 2], P('ident'), may hold values from 0 to 255, as said below
- labels: int32 [16, 192], P('ident', 'section'), may hold values from 0 to 524287, as said below
Outputs:
- embed_grad: float32 [16, 192, 512], P('ident', 'section')
The draws below stay inside these ranges and needn't reach their ends.
Inputs may be any that keep to these rules, and one draw needn't show every extreme that they name: `sampled`: the 2 block numbers of one shard are distinct. `labels`: every label is i * 256 * 128 + sampled[i, a] 128 + t for some shard i, slot a and position t.
All inputs are finite; a program needn't handle non-finite values.
Results may differ from the reference program's by a relative error of at most 0.008.
Values may be sent and summed in bfloat16 or wider, within the bound.
A program may use at most 64 MiB of HBM per device.

```python
import math
import jax
import jax.numpy as jnp
from jax import lax

D = 1024
E = 512
SUB = 3
BLK = 128
BLOCKS_DEV = 256
SAMP_DEV = 2
ROWS = 192
N_SECTION = 2
N_IDENT = 16


def pick_blocks(key):
    shard_keys = jax.random.split(jax.random.fold_in(key, 11), N_IDENT)

    def order_one(shard_key):
        return jax.random.permutation(shard_key, BLOCKS_DEV)
    orders = jax.vmap(order_one)(shard_keys)
    return orders[:, :SAMP_DEV].astype(jnp.int32)


def draw_sampled(key, part):
    return pick_blocks(key)


def draw_labels(key, part):
    chosen = pick_blocks(key)
    owner = jax.random.randint(jax.random.fold_in(key, 21), (N_IDENT, ROWS), 0, N_IDENT)
    slot_pick = jax.random.randint(jax.random.fold_in(key, 22), (N_IDENT, ROWS), 0, SAMP_DEV)
    offset = jax.random.randint(jax.random.fold_in(key, 23), (N_IDENT, ROWS), 0, BLK)
    block_pick = chosen[owner, slot_pick]
    return (owner * (BLOCKS_DEV * BLK) + block_pick * BLK + offset).astype(jnp.int32)


def steps_of(own_key, dims, pieces, least, high):
    factor_of, own = 1.0, jax.random.fold_in(own_key, 6)
    for position, blocks in pieces:
        draws = jnp.exp(jax.random.uniform(jax.random.fold_in(own, position), (blocks,), jnp.float32, least / len(pieces), high / len(pieces)))
        factor_of = factor_of * jnp.repeat(draws, dims[position] // blocks).reshape([-1 if axis == position else 1 for axis in range(len(dims))])
    return factor_of


def bell_draw(key, dims, deviation, reach, pieces=(), held_as=jnp.bfloat16):
    drawn = deviation * jax.random.normal(key, dims, jnp.float32)
    if pieces:
        drawn = drawn * steps_of(key, dims, pieces, -0.22, 0.18)
    return jnp.clip(drawn, -reach, reach).astype(held_as)


def setup_inputs(seed: int = 0) -> dict:
    arg_keys = jax.random.split(jax.random.key(seed), 8)
    inputs = bell_draw(arg_keys[0], (N_IDENT, ROWS, D), 1.0, 6.0, ((0, 16),))
    section_weight = bell_draw(arg_keys[1], (N_SECTION, D, D), D ** -0.5, 0.1875, ((0, 2),))
    section_gain = jnp.clip(1.0 + 0.15 * jax.random.normal(arg_keys[2], (N_SECTION, D), jnp.float32), 0.25, 1.75)
    neck_weight = bell_draw(arg_keys[3], (D, E), D ** -0.5, 0.1875)
    centers = bell_draw(arg_keys[4], (N_IDENT, SAMP_DEV, SUB, BLK, E), 1.0, 6.0, ((0, 16),))
    sampled = draw_sampled(jax.random.fold_in(arg_keys[7], 71), 0)
    labels = draw_labels(jax.random.fold_in(arg_keys[7], 71), 0)
    return {"inputs": inputs, "section_weight": section_weight, "section_gain": section_gain, "neck_weight": neck_weight, "centers": centers, "sampled": sampled, "labels": labels}


logit_scale = 64.0
pool_temp = 0.1
margin_angle = 0.5
sine_offset = 1.05

def layer_norm(values, gain):
    valf = values.astype(jnp.float32)
    center = valf - lax.optimization_barrier(jnp.mean(valf, axis=-1, keepdims=True))
    spread = lax.optimization_barrier(jnp.mean(center * center, axis=-1, keepdims=True))
    return center * lax.rsqrt(spread + 1e-06) * gain

def section_apply(trunk, weight, gain):
    normed = layer_norm(trunk, gain).astype(jnp.bfloat16)
    mixed = jnp.dot(normed, weight, preferred_element_type=jnp.float32)
    return (trunk.astype(jnp.float32) + jax.nn.gelu(mixed, approximate=False)).astype(jnp.bfloat16)

def unit_rows(values):
    valf = values.astype(jnp.float32)
    inverse = lax.rsqrt(lax.optimization_barrier(jnp.sum(valf * valf, axis=-1, keepdims=True)) + 1e-06)
    return (valf * inverse, inverse)

def shard_scores(feature, label_flat, unit_centers, picks, shard, nsamp, nsub, nblk):
    cosine = jnp.dot(feature, unit_centers.T, preferred_element_type=jnp.float32)
    cosine = cosine.reshape(feature.shape[0], nsamp, nsub, nblk)
    expo = jnp.exp(cosine / pool_temp)
    summed = lax.optimization_barrier(jnp.sum(expo, axis=2))
    pooled = pool_temp * jnp.log(summed / nsub)
    weights = expo / summed[:, :, None, :]
    idents = shard * (BLOCKS_DEV * nblk) + picks[:, None] * nblk + jnp.arange(nblk, dtype=jnp.int32)[None, :]
    target = label_flat[:, None, None] == idents[None, :, :]
    root_term = jnp.sqrt(sine_offset - pooled * pooled)
    margin = pooled * math.cos(margin_angle) - root_term * math.sin(margin_angle)
    logits = logit_scale * jnp.where(target, margin, pooled)
    slope = jnp.where(target, math.cos(margin_angle) + pooled * math.sin(margin_angle) / root_term, 1.0)
    return (logits, weights, target, slope)

def reference(inputs, section_weight, section_gain, neck_weight, centers, sampled, labels):
    nsamp = centers.shape[1]
    nsub = centers.shape[2]
    nblk = centers.shape[3]
    width = centers.shape[4]
    trunk = inputs.reshape(-1, inputs.shape[-1])
    for section in range(N_SECTION):
        trunk = section_apply(trunk, section_weight[section], section_gain[section])
    neck_in = layer_norm(trunk, 1.0).astype(jnp.bfloat16)
    embed = jnp.dot(neck_in, neck_weight, preferred_element_type=jnp.float32).astype(jnp.bfloat16)
    direction, inverse = unit_rows(embed)
    unit_embed = direction.astype(jnp.bfloat16)
    label_flat = labels.reshape(-1)
    shard_ids = jnp.arange(centers.shape[0], dtype=jnp.int32)

    def prepare(block):
        return unit_rows(block.reshape(-1, width))[0].astype(jnp.bfloat16)

    def total_step(carry, items):
        block, picks, shard = items
        logits = shard_scores(unit_embed, label_flat, prepare(block), picks, shard, nsamp, nsub, nblk)[0]
        return (carry + lax.optimization_barrier(jnp.sum(jnp.exp(logits), axis=(1, 2))), None)
    totals, _ = lax.scan(total_step, jnp.zeros((unit_embed.shape[0],), jnp.float32), (centers, sampled, shard_ids))

    def grad_step(carry, items):
        block, picks, shard = items
        unit_centers = prepare(block)
        logits, weights, target, slope = shard_scores(unit_embed, label_flat, unit_centers, picks, shard, nsamp, nsub, nblk)
        prob = jnp.exp(logits) / totals[:, None, None]
        factor = logit_scale * (prob - target.astype(jnp.float32)) * slope
        pulled = (factor[:, :, None, :] * weights).astype(jnp.bfloat16).reshape(unit_embed.shape[0], -1)
        return (carry + jnp.dot(pulled, unit_centers, preferred_element_type=jnp.float32), None)
    unit_grad, _ = lax.scan(grad_step, jnp.zeros((unit_embed.shape[0], width), jnp.float32), (centers, sampled, shard_ids))
    along = lax.optimization_barrier(jnp.sum(unit_grad * direction, axis=-1, keepdims=True))
    embed_grad = inverse * (unit_grad - along * direction)
    return embed_grad.reshape(inputs.shape[0], inputs.shape[1], width)
```

```python
import functools
import math

import jax
import jax.numpy as jnp
from jax import lax
from jax.experimental import pallas as pl
from jax.experimental.pallas import tpu as pltpu
from jax.sharding import PartitionSpec as P

BLOCKS_DEV = 256

logit_scale = 64.0
pool_temp = 0.1
margin_angle = 0.5
sine_offset = 1.05

MESH = pl.DeviceIdType.MESH


def split_of(count):
    cores = 2 if count % 2 == 0 else 1
    chips = count // cores
    x = 1
    while (2 * x) * (2 * x) <= chips and chips % (2 * x) == 0:
        x *= 2
    return chips // x, x, cores


def layer_norm(valf):
    center = valf - jnp.mean(valf, axis=-1, keepdims=True)
    spread = jnp.mean(center * center, axis=-1, keepdims=True)
    return center * lax.rsqrt(spread + 1e-06)


def kernel(
    sections, Z, X, C,
    trunk_hbm, weight_hbm, gain_ref, neck_hbm, centers_hbm, sampled_ref, labels_ref,
    out_ref,
    trunk, weight, neck, centers, unit, hid_out, emb_send, emb, feats, labs, lab_tmp,
    expo, coef_a, coef_b, tparts, tsum, pulled, gown, gsend, recv_t, send_x, recv_x, send_z, recv_z,
    local_sem, hid_send_sem, hid_recv_sem, emb_send_sem, emb_recv_sem,
    lab_send_sem, lab_recv_sem, t_send_sem, t_recv_sem,
    fz_send_sem, fx_send_sem, fc_send_sem, f_recv_sem,
    gc_send_sem, gc_recv_sem, gx_send_sem, gx_recv_sem, gz_send_sem, gz_recv_sem,
):
    n = Z * X * C
    pair = 2 if Z % 2 == 0 else 1
    NP = Z // pair
    G = pair * C
    s = lax.axis_index("section")
    me = lax.axis_index("ident")
    c = lax.rem(me, C)
    x = lax.rem(me // C, X)
    z = me // (C * X)
    rows, width = emb.shape
    nsamp, nsub, nblk = expo.shape[1], expo.shape[2], expo.shape[3]
    lanes = G * rows

    def ident_of(zz, xx, cc):
        return (zz * X + xx) * C + cc

    def slot_of(zz, xx, cc):
        return (xx * Z + zz) * C + cc

    in_copy = pltpu.make_async_copy(trunk_hbm, trunk, local_sem.at[0])
    weight_copy = pltpu.make_async_copy(weight_hbm, weight, local_sem.at[1])
    neck_copy = pltpu.make_async_copy(neck_hbm, neck, local_sem.at[2])
    centers_copy = pltpu.make_async_copy(centers_hbm, centers, local_sem.at[3])

    @pl.when(s == 0)
    def _():
        in_copy.start()

    weight_copy.start()

    @pl.when(s == sections - 1)
    def _():
        neck_copy.start()

    centers_copy.start()

    barrier = pltpu.get_barrier_semaphore()

    @pl.loop(1, n)
    def _(d):
        pl.semaphore_signal(
            barrier, inc=1, device_id=(s, lax.rem(me + d, n)), device_id_type=MESH
        )

    for d in range(1, sections):
        pl.semaphore_signal(
            barrier, inc=1, device_id=(lax.rem(s + d, sections), me), device_id_type=MESH
        )

    place = lax.rem(z, pair) * C + c
    lab_tmp[...] = jnp.zeros_like(lab_tmp)
    lab_tmp[0:1, 0:rows] = labels_ref[...]
    labs[me] = pltpu.roll(lab_tmp[...], place * rows, 1)

    pl.semaphore_wait(barrier, n - 1 + sections - 1)

    def lab_copy(peer, index):
        return pltpu.make_async_remote_copy(
            src_ref=labs.at[me], dst_ref=labs.at[me],
            send_sem=lab_send_sem.at[index], recv_sem=lab_recv_sem.at[me],
            device_id=(s, peer), device_id_type=MESH,
        )

    def prepare_centers():
        centers_copy.wait()
        step = 64

        @pl.loop(0, centers.shape[0] // step)
        def _(i):
            at = pl.ds(pl.multiple_of(i * step, step), step)
            valf = centers[at, :].astype(jnp.float32)
            inv = lax.rsqrt(jnp.sum(valf * valf, axis=-1, keepdims=True) + 1e-06)
            unit[at, :] = (valf * inv).astype(jnp.bfloat16)

    def send_labels():
        @pl.loop(1, n)
        def _(d):
            lab_copy(lax.rem(me + d, n), d).start()

    @pl.when(s > 0)
    def _():
        send_labels()
        prepare_centers()

    weight_copy.wait()

    @pl.when(s == 0)
    def _():
        in_copy.wait()

    @pl.when(s == sections - 1)
    def _():
        neck_copy.wait()

    def hid_copy(j):
        return pltpu.make_async_remote_copy(
            src_ref=hid_out.at[j], dst_ref=trunk.at[j],
            send_sem=hid_send_sem.at[j], recv_sem=hid_recv_sem.at[j],
            device_id=(lax.rem(s + 1, sections), me), device_id_type=MESH,
        )

    def emb_copy(j):
        return pltpu.make_async_remote_copy(
            src_ref=emb_send.at[j], dst_ref=emb,
            send_sem=emb_send_sem.at[j], recv_sem=emb_recv_sem,
            device_id=(j, me), device_id_type=MESH,
        )

    for j in range(sections):
        @pl.when(s > 0)
        def _():
            hid_copy(j).wait_recv()

        valf = trunk[j].astype(jnp.float32)
        normed = (layer_norm(valf) * gain_ref[...]).astype(jnp.bfloat16)
        mixed = jnp.dot(normed, weight[...], preferred_element_type=jnp.float32)
        act = mixed * (lax.erf(mixed * (1.0 / math.sqrt(2.0))) + 1.0) * 0.5
        hid_out[j] = (valf + act).astype(jnp.bfloat16)

        @pl.when(s < sections - 1)
        def _():
            hid_copy(j).start()

        @pl.when(s == sections - 1)
        def _():
            neck_in = layer_norm(hid_out[j].astype(jnp.float32)).astype(jnp.bfloat16)
            embed = jnp.dot(neck_in, neck[...], preferred_element_type=jnp.float32)
            if j == sections - 1:
                emb[...] = embed.astype(jnp.bfloat16)
            else:
                emb_send[j] = embed.astype(jnp.bfloat16)
                emb_copy(j).start()

    @pl.when(s == 0)
    def _():
        send_labels()
        prepare_centers()

    @pl.when(s < sections - 1)
    def _():
        emb_copy(0).wait_recv()

    valf = emb[...].astype(jnp.float32)
    inverse = lax.rsqrt(jnp.sum(valf * valf, axis=-1, keepdims=True) + 1e-06)
    feats[slot_of(z, x, c)] = (valf * inverse).astype(jnp.bfloat16)

    def push(slot, send_sem, device):
        return pltpu.make_async_remote_copy(
            src_ref=feats.at[slot], dst_ref=feats.at[slot],
            send_sem=send_sem, recv_sem=f_recv_sem.at[slot],
            device_id=(s, device), device_id_type=MESH,
        )

    def z_send(d):
        zz = lax.rem(z + d, Z)
        return push(slot_of(z, x, c), fz_send_sem.at[d], ident_of(zz, x, c))

    def x_send(zz, d):
        xx = lax.rem(x + d, X)
        return push(slot_of(zz, x, c), fx_send_sem.at[zz, d], ident_of(z, xx, c))

    def c_send(zz, xx, d):
        cc = lax.rem(c + d, C)
        return push(slot_of(zz, xx, c), fc_send_sem.at[xx * Z + zz, d], ident_of(z, x, cc))

    def arrived(zz, xx, cc):
        push(slot_of(zz, xx, cc), fz_send_sem.at[0], me).wait_recv()

    def others(p, first):
        base = lax.rem(z // pair + p, NP) * pair
        return [base + lax.rem(lax.rem(z, pair) + j, pair) for j in range(pair)][first:]

    for d in range(1, Z):
        z_send(d).start()
    for d in range(1, X):
        x_send(z, d).start()
    for d in range(1, C):
        c_send(z, x, d).start()

    lane_index = lax.broadcasted_iota(jnp.int32, (16, lanes), 0)
    cos_m, sin_m = math.cos(margin_angle), math.sin(margin_angle)

    def forward_scores(p, xx):
        pr = lax.rem(z // pair + p, NP)
        ch = xx * NP + pr
        block = feats[pl.ds(ch * G, G)].reshape(lanes, width)
        lab = None
        for j in range(pair):
            for cc in range(C):
                one = labs[ident_of(pr * pair + j, xx, cc)]
                lab = one if lab is None else lab + one
        lab = jnp.broadcast_to(lab[0:1], (16, lanes))
        total = jnp.zeros((16, lanes), jnp.float32)
        for a in range(nsamp):
            cosines = []
            for k in range(nsub):
                cosines.append(lax.dot_general(
                    unit[(a * nsub + k) * nblk:(a * nsub + k + 1) * nblk, :], block,
                    (((1,), (1,)), ((), ())), preferred_element_type=jnp.float32,
                ))
            first = me * (BLOCKS_DEV * nblk) + sampled_ref[0, a] * nblk
            for r in range(0, nblk, 16):
                exps = [jnp.exp(cosines[k][r:r + 16] * (1.0 / pool_temp)) for k in range(nsub)]
                summed = exps[0]
                for k in range(1, nsub):
                    summed = summed + exps[k]
                pooled = pool_temp * jnp.log(summed * (1.0 / nsub))
                target = lab == (first + r + lane_index)
                gap = sine_offset - pooled * pooled
                rroot = lax.rsqrt(gap)
                logits = logit_scale * jnp.where(
                    target, pooled * cos_m - gap * rroot * sin_m, pooled
                )
                slope = jnp.where(target, cos_m + pooled * sin_m * rroot, 1.0)
                el = jnp.exp(logits)
                total = total + el
                scaled = logit_scale * slope / summed
                at = slice(r, r + 16)
                coef_a[ch, a, at, :] = el * scaled
                coef_b[ch, a, at, :] = jnp.where(target, scaled, 0.0)
                for k in range(nsub):
                    expo[ch, a, k, at, :] = exps[k].astype(expo.dtype)
        tparts[me, ch] = jnp.sum(total, axis=0, keepdims=True)

    def lab_wait():
        @pl.loop(1, n)
        def _(d):
            peer = lax.rem(me + d, n)
            pltpu.make_async_remote_copy(
                src_ref=labs.at[peer], dst_ref=labs.at[peer],
                send_sem=lab_send_sem.at[0], recv_sem=lab_recv_sem.at[peer],
                device_id=(s, peer), device_id_type=MESH,
            ).wait_recv()

    lab_wait()
    for p in range(NP):
        for zz in others(p, 1 if p == 0 else 0):
            arrived(zz, x, c)
            for d in range(1, X):
                x_send(zz, d).start()
            for d in range(1, C):
                c_send(zz, x, d).start()
        for zz in others(p, 0):
            for d in range(1, C):
                arrived(zz, x, lax.rem(c + d, C))
        forward_scores(p, x)
    for dx in range(1, X):
        xx = lax.rem(x + dx, X)
        for p in range(NP):
            for zz in others(p, 0):
                arrived(zz, xx, c)
                for d in range(1, C):
                    c_send(zz, xx, d).start()
            for zz in others(p, 0):
                for d in range(1, C):
                    arrived(zz, xx, lax.rem(c + d, C))
            forward_scores(p, xx)

    def t_copy(src, peer, index):
        return pltpu.make_async_remote_copy(
            src_ref=tparts.at[src], dst_ref=tparts.at[src],
            send_sem=t_send_sem.at[index], recv_sem=t_recv_sem.at[src],
            device_id=(s, peer), device_id_type=MESH,
        )

    @pl.loop(1, n)
    def _(d):
        t_copy(me, lax.rem(me + d, n), d).start()

    @pl.loop(1, n)
    def _(d):
        peer = lax.rem(me + d, n)
        t_copy(peer, peer, 0).wait_recv()

    tsum[...] = 1.0 / jnp.sum(tparts[...], axis=0)

    def gc_copy(zz, xx, d):
        cc = lax.rem(c + d, C)
        return pltpu.make_async_remote_copy(
            src_ref=gsend.at[slot_of(zz, xx, cc)], dst_ref=recv_t.at[xx * Z + zz, c],
            send_sem=gc_send_sem.at[slot_of(zz, xx, cc)], recv_sem=gc_recv_sem.at[xx * Z + zz, c],
            device_id=(s, ident_of(z, x, cc)), device_id_type=MESH,
        )

    def gc_arrived(zz, xx, cc):
        pltpu.make_async_remote_copy(
            src_ref=recv_t.at[xx * Z + zz, cc], dst_ref=recv_t.at[xx * Z + zz, cc],
            send_sem=gc_send_sem.at[0], recv_sem=gc_recv_sem.at[xx * Z + zz, cc],
            device_id=(s, me), device_id_type=MESH,
        ).wait_recv()

    def gx_copy(zz, xx):
        return pltpu.make_async_remote_copy(
            src_ref=send_x.at[xx * Z + zz], dst_ref=recv_x.at[x * Z + zz],
            send_sem=gx_send_sem.at[xx * Z + zz], recv_sem=gx_recv_sem.at[x * Z + zz],
            device_id=(s, ident_of(z, xx, c)), device_id_type=MESH,
        )

    def gz_copy(zz):
        return pltpu.make_async_remote_copy(
            src_ref=send_z.at[zz], dst_ref=recv_z.at[z],
            send_sem=gz_send_sem.at[zz], recv_sem=gz_recv_sem.at[z],
            device_id=(s, ident_of(zz, x, c)), device_id_type=MESH,
        )

    def backward(p, xx):
        pr = lax.rem(z // pair + p, NP)
        ch = xx * NP + pr
        inv_total = jnp.broadcast_to(tsum[ch], (16, lanes))
        for a in range(nsamp):
            for r in range(0, nblk, 16):
                at = slice(r, r + 16)
                factor = coef_a[ch, a, at, :] * inv_total - coef_b[ch, a, at, :]
                for k in range(nsub):
                    first = (a * nsub + k) * nblk + r
                    pulled[first:first + 16, :] = (
                        factor * expo[ch, a, k, at, :].astype(jnp.float32)
                    ).astype(jnp.bfloat16)
        grad = lax.dot_general(
            pulled[...], unit[...], (((0,), (0,)), ((), ())), preferred_element_type=jnp.float32
        ).reshape(G, rows, width)
        gown[pl.ds(ch * G, G)] = grad
        gsend[pl.ds(ch * G, G)] = grad.astype(jnp.bfloat16)
        for zz in others(p, 0):
            for d in range(1, C):
                gc_copy(zz, xx, d).start()

    def core_sum(zz, xx):
        value = gown[slot_of(zz, xx, c)]
        for d in range(1, C):
            cc = lax.rem(c + d, C)
            gc_arrived(zz, xx, cc)
            value = value + recv_t[xx * Z + zz, cc].astype(jnp.float32)
        return value

    def reduce_step(p, dx):
        if dx:
            xx = lax.rem(x + dx, X)
            for zz in others(p, 0):
                send_x[xx * Z + zz] = core_sum(zz, xx).astype(jnp.bfloat16)
                gx_copy(zz, xx).start()
            return None
        mine = None
        order = others(p, 0)
        for zz in (order[1:] + order[:1]) if p == 0 else order:
            value = core_sum(zz, x)
            for d in range(1, X):
                xx = lax.rem(x + d, X)
                pltpu.make_async_remote_copy(
                    src_ref=send_x.at[xx * Z + zz], dst_ref=recv_x.at[xx * Z + zz],
                    send_sem=gx_send_sem.at[xx * Z + zz], recv_sem=gx_recv_sem.at[xx * Z + zz],
                    device_id=(s, me), device_id_type=MESH,
                ).wait_recv()
                value = value + recv_x[xx * Z + zz].astype(jnp.float32)
            if p == 0 and zz is order[0]:
                mine = value
            else:
                send_z[zz] = value.astype(jnp.bfloat16)
                gz_copy(zz).start()
        return mine

    plan = [(p, dx) for dx in list(range(1, X)) + [0] for p in reversed(range(NP))]
    for i, (p, dx) in enumerate(plan):
        backward(p, lax.rem(x + dx, X))
        if i:
            reduce_step(*plan[i - 1])
    own_grad = reduce_step(*plan[-1])

    for d in range(1, Z):
        zz = lax.rem(z + d, Z)
        pltpu.make_async_remote_copy(
            src_ref=send_z.at[zz], dst_ref=recv_z.at[zz],
            send_sem=gz_send_sem.at[zz], recv_sem=gz_recv_sem.at[zz],
            device_id=(s, me), device_id_type=MESH,
        ).wait_recv()
        own_grad = own_grad + recv_z[zz].astype(jnp.float32)

    valf = emb[...].astype(jnp.float32)
    inverse = lax.rsqrt(jnp.sum(valf * valf, axis=-1, keepdims=True) + 1e-06)
    direction = valf * inverse
    along = jnp.sum(own_grad * direction, axis=-1, keepdims=True)
    out_ref[0] = inverse * (own_grad - along * direction)

    for j in range(sections):
        @pl.when(s < sections - 1)
        def _():
            hid_copy(j).wait_send()

        if j < sections - 1:
            @pl.when(s == sections - 1)
            def _():
                emb_copy(j).wait_send()

    @pl.loop(1, n)
    def _(d):
        lab_copy(lax.rem(me + d, n), d).wait_send()
        t_copy(me, lax.rem(me + d, n), d).wait_send()

    for d in range(1, Z):
        z_send(d).wait_send()
    for j in range(Z):
        zz = lax.rem(z + j, Z)
        for d in range(1, X):
            x_send(zz, d).wait_send()
            gx_copy(zz, lax.rem(x + d, X)).wait_send()
        if j:
            gz_copy(zz).wait_send()
        for i in range(X):
            for d in range(1, C):
                c_send(zz, lax.rem(x + i, X), d).wait_send()
                gc_copy(zz, lax.rem(x + i, X), d).wait_send()


def shards(Z, X, C, inputs, section_weight, section_gain, neck_weight, centers, sampled, labels):
    sections = lax.axis_size("section")
    n = Z * X * C
    dim = inputs.shape[-1]
    rows = inputs.shape[1] // sections
    _, nsamp, nsub, nblk, width = centers.shape
    pair = 2 if Z % 2 == 0 else 1
    group = pair * C
    chunks = n // group
    lanes = group * rows
    total_rows = n * rows
    bf16, f32 = jnp.bfloat16, jnp.float32
    expo_type = f32 if total_rows * nsamp * nsub * nblk * 4 <= 8 * 2**20 else bf16
    dma = pltpu.SemaphoreType.DMA
    vmem = pltpu.VMEM
    flat = centers.reshape(-1, width)
    scratch = [
        vmem((sections, rows, dim), bf16),
        vmem(section_weight.shape[1:], bf16),
        vmem(neck_weight.shape, bf16),
        vmem(flat.shape, bf16),
        vmem(flat.shape, bf16),
        vmem((sections, rows, dim), bf16),
        vmem((sections, rows, width), bf16),
        vmem((rows, width), bf16),
        vmem((n, rows, width), bf16),
        vmem((n, 8, lanes), jnp.int32),
        vmem((8, lanes), jnp.int32),
        vmem((chunks, nsamp, nsub, nblk, lanes), expo_type),
        vmem((chunks, nsamp, nblk, lanes), f32),
        vmem((chunks, nsamp, nblk, lanes), f32),
        vmem((n, chunks, 1, lanes), f32),
        vmem((chunks, 1, lanes), f32),
        vmem((nsamp * nsub * nblk, lanes), bf16),
        vmem((n, rows, width), f32),
        vmem((n, rows, width), bf16),
        vmem((X * Z, C, rows, width), bf16),
        vmem((X * Z, rows, width), bf16),
        vmem((X * Z, rows, width), bf16),
        vmem((Z, rows, width), bf16),
        vmem((Z, rows, width), bf16),
        dma((4,)), dma((sections,)), dma((sections,)), dma((sections,)), dma,
        dma((n,)), dma((n,)), dma((n,)), dma((n,)),
        dma((Z,)), dma((Z, X)), dma((X * Z, C)), dma((n,)),
        dma((n,)), dma((X * Z, C)), dma((X * Z,)), dma((X * Z,)), dma((Z,)), dma((Z,)),
    ]
    any_spec = pl.BlockSpec(memory_space=pl.ANY)
    vmem_spec = pl.BlockSpec(memory_space=pltpu.VMEM)
    smem_spec = pl.BlockSpec(memory_space=pltpu.SMEM)
    return pl.pallas_call(
        functools.partial(kernel, sections, Z, X, C),
        out_shape=jax.ShapeDtypeStruct((1, rows, width), f32),
        in_specs=[any_spec, any_spec, vmem_spec, any_spec, any_spec, smem_spec, vmem_spec],
        out_specs=vmem_spec,
        scratch_shapes=scratch,
        compiler_params=pltpu.CompilerParams(
            collective_id=0, has_side_effects=True, vmem_limit_bytes=62 * 2**20
        ),
        name="arcface_head",
    )(
        inputs.reshape(sections, rows, dim), section_weight[0], section_gain, neck_weight,
        flat, sampled, labels,
    )


def solution(mesh):
    Z, X, C = split_of(mesh.shape["ident"])
    in_specs = (
        P("ident", None, None),
        P("section", None, None),
        P("section", None),
        P(),
        P("ident", None, None, None, None),
        P("ident", None),
        P("ident", "section"),
    )
    out_specs = P("ident", "section", None)
    return jax.shard_map(
        functools.partial(shards, Z, X, C),
        mesh=mesh, in_specs=in_specs, out_specs=out_specs, check_vma=False,
    )
```

```python
import functools
import math

import jax
import jax.numpy as jnp
from jax import lax
from jax.experimental import pallas as pl
from jax.experimental.pallas import tpu as pltpu
from jax.sharding import PartitionSpec as P

BLOCKS_DEV = 256

logit_scale = 64.0
pool_temp = 0.1
margin_angle = 0.5
sine_offset = 1.05

MESH = pl.DeviceIdType.MESH


def split_of(count):
    cores = 2 if count % 2 == 0 else 1
    chips = count // cores
    x = 1
    while (2 * x) * (2 * x) <= chips and chips % (2 * x) == 0:
        x *= 2
    return chips // x, x, cores


def layer_norm(valf):
    center = valf - jnp.mean(valf, axis=-1, keepdims=True)
    spread = jnp.mean(center * center, axis=-1, keepdims=True)
    return center * lax.rsqrt(spread + 1e-06)


def kernel(
    sections, Z, X, C,
    trunk_hbm, weight_hbm, gain_ref, neck_hbm, centers_hbm, sampled_ref, labels_ref,
    out_ref,
    trunk, weight, neck, raw, unit, hid_out, emb_send, emb, feats, labs, idents,
    expo, coef_a, coef_b, tparts, tsum, pulled, send_z, recv_z,
    local_sem, hid_send_sem, hid_recv_sem, emb_send_sem, emb_recv_sem,
    id_send_sem, id_recv_sem, lab_send_sem, lab_recv_sem, t_send_sem, t_recv_sem,
    rx_send_sem, rc_send_sem, r_recv_sem, f_send_sem, f_recv_sem, g_send_sem, g_recv_sem,
):
    Q = X * C
    s = lax.axis_index("section")
    me = lax.axis_index("ident")
    c = lax.rem(me, C)
    x = lax.rem(me // C, X)
    z = me // Q
    mine = x * C + c
    rows, width = emb.shape
    lanes = feats.shape[1]
    nsamp, nsub, nblk = expo.shape[2], expo.shape[3], expo.shape[4]
    per_slot = nsub * nblk

    def in_row(q):
        return (s, z * Q + q)

    def at_z(zz):
        return (s, zz * Q + mine)

    def remote(src, dst, send_sem, recv_sem, device):
        return pltpu.make_async_remote_copy(
            src_ref=src, dst_ref=dst, send_sem=send_sem, recv_sem=recv_sem,
            device_id=device, device_id_type=MESH,
        )

    in_copy = pltpu.make_async_copy(trunk_hbm, trunk, local_sem.at[0])
    weight_copy = pltpu.make_async_copy(weight_hbm, weight, local_sem.at[1])
    neck_copy = pltpu.make_async_copy(neck_hbm, neck, local_sem.at[2])
    centers_copy = pltpu.make_async_copy(centers_hbm, raw.at[mine], local_sem.at[3])

    @pl.when(s == 0)
    def _():
        in_copy.start()

    weight_copy.start()

    @pl.when(s == sections - 1)
    def _():
        neck_copy.start()

    centers_copy.start()

    if lanes > rows:
        feats[:, rows:lanes, :] = jnp.zeros((Z, lanes - rows, width), jnp.bfloat16)

    barrier = pltpu.get_barrier_semaphore()
    for d in range(1, Z):
        pl.semaphore_signal(barrier, inc=1, device_id=at_z(lax.rem(z + d, Z)), device_id_type=MESH)
    for d in range(1, Q):
        pl.semaphore_signal(barrier, inc=1, device_id=in_row(lax.rem(mine + d, Q)), device_id_type=MESH)
    for d in range(1, sections):
        pl.semaphore_signal(
            barrier, inc=1, device_id=(lax.rem(s + d, sections), me), device_id_type=MESH
        )

    labs[z] = jnp.full(labs.shape[1:], -1, jnp.int32)
    labs[z, 0:1, 0:rows] = labels_ref[...]
    for a in range(nsamp):
        first = me * (BLOCKS_DEV * nblk) + sampled_ref[0, a] * nblk
        idents[mine, a] = jnp.full((1, lanes), first, jnp.int32)

    pl.semaphore_wait(barrier, Z - 1 + Q - 1 + sections - 1)

    def half(a):
        return pl.ds(a * per_slot, per_slot)

    def rx_copy(d, a):
        xx = lax.rem(x + d, X)
        return remote(
            centers_hbm.at[half(a)], raw.at[mine, half(a)],
            rx_send_sem.at[d, a], r_recv_sem.at[mine, a], in_row(xx * C + c),
        )

    def rc_own(d, a):
        cc = lax.rem(c + d, C)
        return remote(
            centers_hbm.at[half(a)], raw.at[mine, half(a)],
            rc_send_sem.at[x, d, a], r_recv_sem.at[mine, a], in_row(x * C + cc),
        )

    def rc_forward(xx, d, a):
        cc = lax.rem(c + d, C)
        q = xx * C + c
        return remote(
            raw.at[q, half(a)], raw.at[q, half(a)],
            rc_send_sem.at[xx, d, a], r_recv_sem.at[q, a], in_row(x * C + cc),
        )

    def r_arrived(q, a):
        remote(
            raw.at[q, half(a)], raw.at[q, half(a)],
            rc_send_sem.at[0, 0, a], r_recv_sem.at[q, a], in_row(mine),
        ).wait_recv()

    def id_copy(src, q, index):
        return remote(
            idents.at[src], idents.at[src], id_send_sem.at[index], id_recv_sem.at[src], in_row(q)
        )

    def lab_copy(src, zz, index):
        return remote(
            labs.at[src], labs.at[src], lab_send_sem.at[index], lab_recv_sem.at[src], at_z(zz)
        )

    for a in range(nsamp):
        for d in range(1, X):
            rx_copy(d, a).start()
    for a in range(nsamp):
        for d in range(1, C):
            rc_own(d, a).start()
    for d in range(1, Q):
        id_copy(mine, lax.rem(mine + d, Q), d).start()
    for d in range(1, Z):
        lab_copy(z, lax.rem(z + d, Z), d).start()

    step = 64

    def prepare(q):
        @pl.loop(0, raw.shape[1] // step)
        def _(i):
            at = pl.ds(pl.multiple_of(i * step, step), step)
            valf = raw[q, at, :].astype(jnp.float32)
            inv = lax.rsqrt(jnp.sum(valf * valf, axis=-1, keepdims=True) + 1e-06)
            unit[q, at, :] = (valf * inv).astype(jnp.bfloat16)

    def prepare_chip():
        centers_copy.wait()
        prepare(mine)
        for d in range(1, C):
            q = x * C + lax.rem(c + d, C)
            for a in range(nsamp):
                r_arrived(q, a)
            prepare(q)

    @pl.when(s > 0)
    def _():
        prepare_chip()

    weight_copy.wait()

    @pl.when(s == 0)
    def _():
        in_copy.wait()

    @pl.when(s == sections - 1)
    def _():
        neck_copy.wait()

    def hid_copy(j):
        return remote(
            hid_out.at[j], trunk.at[j], hid_send_sem.at[j], hid_recv_sem.at[j],
            (lax.rem(s + 1, sections), me),
        )

    def emb_copy(j):
        return remote(emb_send.at[j], emb, emb_send_sem.at[j], emb_recv_sem, (j, me))

    for j in range(sections):
        @pl.when(s > 0)
        def _():
            hid_copy(j).wait_recv()

        valf = trunk[j].astype(jnp.float32)
        normed = (layer_norm(valf) * gain_ref[...]).astype(jnp.bfloat16)
        mixed = jnp.dot(normed, weight[...], preferred_element_type=jnp.float32)
        act = mixed * (lax.erf(mixed * (1.0 / math.sqrt(2.0))) + 1.0) * 0.5
        hid_out[j] = (valf + act).astype(jnp.bfloat16)

        @pl.when(s < sections - 1)
        def _():
            hid_copy(j).start()

        @pl.when(s == sections - 1)
        def _():
            neck_in = layer_norm(hid_out[j].astype(jnp.float32)).astype(jnp.bfloat16)
            embed = jnp.dot(neck_in, neck[...], preferred_element_type=jnp.float32)
            if j == sections - 1:
                emb[...] = embed.astype(jnp.bfloat16)
            else:
                emb_send[j] = embed.astype(jnp.bfloat16)
                emb_copy(j).start()

    @pl.when(s == 0)
    def _():
        prepare_chip()

    @pl.when(s < sections - 1)
    def _():
        emb_copy(0).wait_recv()

    valf = emb[...].astype(jnp.float32)
    inverse = lax.rsqrt(jnp.sum(valf * valf, axis=-1, keepdims=True) + 1e-06)
    feats[z, 0:rows, :] = (valf * inverse).astype(jnp.bfloat16)

    def near(k):
        high = (2 * z) // Z
        low = z + high * (Z - 1 - 2 * z)
        index = k + (k - low + Z) // Z
        return index + high * (Z - 1 - 2 * index)

    def f_copy(src, zz, index):
        part = feats.at[src, pl.ds(0, rows)]
        return remote(part, part, f_send_sem.at[index], f_recv_sem.at[src], at_z(zz))

    for k in range(Z - 1):
        f_copy(z, near(k), k).start()

    for d in range(1, X):
        xx = lax.rem(x + d, X)
        for a in range(nsamp):
            r_arrived(xx * C + c, a)
            for e in range(1, C):
                rc_forward(xx, e, a).start()
    for d in range(1, X):
        xx = lax.rem(x + d, X)
        prepare(xx * C + c)
    for d in range(1, X):
        xx = lax.rem(x + d, X)
        for e in range(1, C):
            q = xx * C + lax.rem(c + e, C)
            for a in range(nsamp):
                r_arrived(q, a)
            prepare(q)
    for d in range(1, Q):
        q = lax.rem(mine + d, Q)
        id_copy(q, q, 0).wait_recv()
    for k in range(Z - 1):
        lab_copy(near(k), near(k), 0).wait_recv()

    tile = 32
    row_index = lax.broadcasted_iota(jnp.int32, (tile, lanes), 0)
    cos_m, sin_m = math.cos(margin_angle), math.sin(margin_angle)

    def scores(zz):
        lab = jnp.broadcast_to(labs[zz, 0:1, :], (tile, lanes)) - row_index

        def shard(q, total):
            for a in range(nsamp):
                cosine = lax.dot_general(
                    unit[q, half(a), :], feats[zz],
                    (((1,), (1,)), ((), ())), preferred_element_type=jnp.float32,
                )
                hit = lab - jnp.broadcast_to(idents[q, a], (tile, lanes))
                for r in range(0, nblk, tile):
                    exps = [
                        jnp.exp(cosine[k * nblk + r:k * nblk + r + tile] * (1.0 / pool_temp))
                        for k in range(nsub)
                    ]
                    summed = exps[0]
                    for k in range(1, nsub):
                        summed = summed + exps[k]
                    pooled = pool_temp * jnp.log(summed * (1.0 / nsub))
                    target = hit == r
                    gap = sine_offset - pooled * pooled
                    rroot = lax.rsqrt(gap)
                    logits = logit_scale * jnp.where(
                        target, pooled * cos_m - gap * rroot * sin_m, pooled
                    )
                    slope = jnp.where(target, cos_m + pooled * sin_m * rroot, 1.0)
                    el = jnp.exp(logits)
                    total = total + el
                    scaled = logit_scale * slope / summed
                    at = slice(r, r + tile)
                    coef_a[zz, q, a, at, :] = el * scaled
                    coef_b[zz, q, a, at, :] = jnp.where(target, scaled, 0.0)
                    for k in range(nsub):
                        expo[zz, q, a, k, at, :] = exps[k].astype(expo.dtype)
            return total

        total = lax.fori_loop(0, Q, shard, jnp.zeros((tile, lanes), jnp.float32))
        tparts[z, zz] = jnp.sum(total, axis=0, keepdims=True)

    scores(z)
    for k in range(Z - 1):
        f_copy(near(k), near(k), 0).wait_recv()
        scores(near(k))

    def t_copy(src, zz, index):
        return remote(
            tparts.at[src], tparts.at[src], t_send_sem.at[index], t_recv_sem.at[src], at_z(zz)
        )

    for k in range(Z - 1):
        t_copy(z, near(k), k).start()
    for k in range(Z - 1):
        t_copy(near(k), near(k), 0).wait_recv()

    tsum[...] = 1.0 / jnp.sum(tparts[...], axis=0)

    def backward(zz):
        inv_total = jnp.broadcast_to(tsum[zz], (tile, lanes))

        @pl.loop(0, Q)
        def _(q):
            for a in range(nsamp):
                for r in range(0, nblk, tile):
                    at = slice(r, r + tile)
                    factor = coef_a[zz, q, a, at, :] * inv_total - coef_b[zz, q, a, at, :]
                    for k in range(nsub):
                        first = (a * nsub + k) * nblk + r
                        pulled[q, first:first + tile, :] = (
                            factor * expo[zz, q, a, k, at, :].astype(jnp.float32)
                        ).astype(jnp.bfloat16)

        grad = lax.dot_general(
            pulled[...].reshape(-1, lanes), unit[...].reshape(-1, width),
            (((0,), (0,)), ((), ())), preferred_element_type=jnp.float32,
        )
        return grad[0:rows]

    def g_copy(zz):
        return remote(
            send_z.at[zz], recv_z.at[z], g_send_sem.at[zz], g_recv_sem.at[z], at_z(zz)
        )

    for k in reversed(range(Z - 1)):
        send_z[near(k)] = backward(near(k)).astype(jnp.bfloat16)
        g_copy(near(k)).start()
    own_grad = backward(z)

    for k in range(Z - 1):
        zz = near(k)
        remote(
            send_z.at[zz], recv_z.at[zz], g_send_sem.at[zz], g_recv_sem.at[zz], at_z(zz)
        ).wait_recv()
        own_grad = own_grad + recv_z[zz].astype(jnp.float32)

    valf = emb[...].astype(jnp.float32)
    inverse = lax.rsqrt(jnp.sum(valf * valf, axis=-1, keepdims=True) + 1e-06)
    direction = valf * inverse
    along = jnp.sum(own_grad * direction, axis=-1, keepdims=True)
    out_ref[0] = inverse * (own_grad - along * direction)

    for j in range(sections):
        @pl.when(s < sections - 1)
        def _():
            hid_copy(j).wait_send()

        if j < sections - 1:
            @pl.when(s == sections - 1)
            def _():
                emb_copy(j).wait_send()

    for d in range(1, Q):
        id_copy(mine, lax.rem(mine + d, Q), d).wait_send()
    for d in range(1, Z):
        lab_copy(z, lax.rem(z + d, Z), d).wait_send()
    for a in range(nsamp):
        for d in range(1, X):
            rx_copy(d, a).wait_send()
            for e in range(1, C):
                rc_forward(lax.rem(x + d, X), e, a).wait_send()
        for d in range(1, C):
            rc_own(d, a).wait_send()
    for k in range(Z - 1):
        f_copy(z, near(k), k).wait_send()
        t_copy(z, near(k), k).wait_send()
        g_copy(near(k)).wait_send()


def shards(Z, X, C, inputs, section_weight, section_gain, neck_weight, centers, sampled, labels):
    sections = lax.axis_size("section")
    Q = X * C
    dim = inputs.shape[-1]
    rows = inputs.shape[1] // sections
    _, nsamp, nsub, nblk, width = centers.shape
    lanes = -(-rows // 128) * 128
    bf16, f32 = jnp.bfloat16, jnp.float32
    expo_type = f32 if Z * lanes * Q * nsamp * nsub * nblk * 4 <= 8 * 2**20 else bf16
    dma = pltpu.SemaphoreType.DMA
    vmem = pltpu.VMEM
    flat = centers.reshape(-1, width)
    scratch = [
        vmem((sections, rows, dim), bf16),
        vmem(section_weight.shape[1:], bf16),
        vmem(neck_weight.shape, bf16),
        vmem((Q,) + flat.shape, bf16),
        vmem((Q,) + flat.shape, bf16),
        vmem((sections, rows, dim), bf16),
        vmem((sections, rows, width), bf16),
        vmem((rows, width), bf16),
        vmem((Z, lanes, width), bf16),
        vmem((Z, 8, lanes), jnp.int32),
        vmem((Q, nsamp, 1, lanes), jnp.int32),
        vmem((Z, Q, nsamp, nsub, nblk, lanes), expo_type),
        vmem((Z, Q, nsamp, nblk, lanes), f32),
        vmem((Z, Q, nsamp, nblk, lanes), f32),
        vmem((Z, Z, 1, lanes), f32),
        vmem((Z, 1, lanes), f32),
        vmem((Q, nsamp * nsub * nblk, lanes), bf16),
        vmem((Z, rows, width), bf16),
        vmem((Z, rows, width), bf16),
        dma((4,)), dma((sections,)), dma((sections,)), dma((sections,)), dma,
        dma((Q,)), dma((Q,)), dma((Z,)), dma((Z,)), dma((Z,)), dma((Z,)),
        dma((X, nsamp)), dma((X, C, nsamp)), dma((Q, nsamp)), dma((Z,)), dma((Z,)),
        dma((Z,)), dma((Z,)),
    ]
    any_spec = pl.BlockSpec(memory_space=pl.ANY)
    vmem_spec = pl.BlockSpec(memory_space=pltpu.VMEM)
    smem_spec = pl.BlockSpec(memory_space=pltpu.SMEM)
    return pl.pallas_call(
        functools.partial(kernel, sections, Z, X, C),
        out_shape=jax.ShapeDtypeStruct((1, rows, width), f32),
        in_specs=[any_spec, any_spec, vmem_spec, any_spec, any_spec, smem_spec, vmem_spec],
        out_specs=vmem_spec,
        scratch_shapes=scratch,
        compiler_params=pltpu.CompilerParams(
            collective_id=0, has_side_effects=True, vmem_limit_bytes=62 * 2**20
        ),
        name="arcface_head",
    )(
        inputs.reshape(sections, rows, dim), section_weight[0], section_gain, neck_weight,
        flat, sampled, labels,
    )


def solution(mesh):
    Z, X, C = split_of(mesh.shape["ident"])
    in_specs = (
        P("ident", None, None),
        P("section", None, None),
        P("section", None),
        P(),
        P("ident", None, None, None, None),
        P("ident", None),
        P("ident", "section"),
    )
    out_specs = P("ident", "section", None)
    return jax.shard_map(
        functools.partial(shards, Z, X, C),
        mesh=mesh, in_specs=in_specs, out_specs=out_specs, check_vma=False,
    )
```

```python
import functools
import math

import jax
import jax.numpy as jnp
from jax import lax
from jax.experimental import pallas as pl
from jax.experimental.pallas import tpu as pltpu
from jax.sharding import PartitionSpec as P

BLOCKS_DEV = 256

logit_scale = 64.0
pool_temp = 0.1
margin_angle = 0.5
sine_offset = 1.05

MESH = pl.DeviceIdType.MESH


def split_of(count):
    cores = 2 if count % 2 == 0 else 1
    chips = count // cores
    x = 1
    while (2 * x) * (2 * x) <= chips and chips % (2 * x) == 0:
        x *= 2
    return chips // x, x, cores


def layer_norm(valf):
    center = valf - jnp.mean(valf, axis=-1, keepdims=True)
    spread = jnp.mean(center * center, axis=-1, keepdims=True)
    return center * lax.rsqrt(spread + 1e-06)


def kernel(
    sections, H, X, W, C,
    trunk_hbm, weight_hbm, gain_ref, neck_hbm, centers_hbm, sampled_ref, labels_ref,
    out_ref,
    trunk, weight, neck, raw, unit, hid_out, emb_send, emb, feats, labs, idents,
    expo, coef_a, coef_b, tparts, tsum, pulled, send_w, recv_w, send_h, recv_h,
    local_sem, hid_send_sem, hid_recv_sem, emb_send_sem, emb_recv_sem,
    id_send_sem, id_recv_sem, lab_send_sem, lab_recv_sem, t_send_sem, t_recv_sem,
    rx_send_sem, rc_send_sem, r_recv_sem, fh_send_sem, fw_send_sem, f_recv_sem,
    gw_send_sem, gw_recv_sem, gh_send_sem, gh_recv_sem,
):
    Q = X * C
    Z = H * W
    s = lax.axis_index("section")
    me = lax.axis_index("ident")
    c = lax.rem(me, C)
    w = lax.rem(me // C, W)
    x = lax.rem(me // (C * W), X)
    h = me // (C * W * X)
    z = h * W + w
    mine = x * C + c
    rows, width = emb.shape
    lanes = feats.shape[1]
    nsamp, nsub, nblk = expo.shape[2], expo.shape[3], expo.shape[4]
    per_slot = nsub * nblk

    def in_row(q):
        return (s, ((h * X + q // C) * W + w) * C + lax.rem(q, C))

    def at_z(zz):
        return (s, ((zz // W * X + x) * W + lax.rem(zz, W)) * C + c)

    def remote(src, dst, send_sem, recv_sem, device):
        return pltpu.make_async_remote_copy(
            src_ref=src, dst_ref=dst, send_sem=send_sem, recv_sem=recv_sem,
            device_id=device, device_id_type=MESH,
        )

    in_copy = pltpu.make_async_copy(trunk_hbm, trunk, local_sem.at[0])
    weight_copy = pltpu.make_async_copy(weight_hbm, weight, local_sem.at[1])
    neck_copy = pltpu.make_async_copy(neck_hbm, neck, local_sem.at[2])
    centers_copy = pltpu.make_async_copy(centers_hbm, raw.at[mine], local_sem.at[3])

    @pl.when(s == 0)
    def _():
        in_copy.start()

    weight_copy.start()

    @pl.when(s == sections - 1)
    def _():
        neck_copy.start()

    centers_copy.start()

    if lanes > rows:
        feats[:, rows:lanes, :] = jnp.zeros((Z, lanes - rows, width), jnp.bfloat16)

    barrier = pltpu.get_barrier_semaphore()
    for d in range(1, Z):
        pl.semaphore_signal(barrier, inc=1, device_id=at_z(lax.rem(z + d, Z)), device_id_type=MESH)
    for d in range(1, Q):
        pl.semaphore_signal(barrier, inc=1, device_id=in_row(lax.rem(mine + d, Q)), device_id_type=MESH)
    for d in range(1, sections):
        pl.semaphore_signal(
            barrier, inc=1, device_id=(lax.rem(s + d, sections), me), device_id_type=MESH
        )

    labs[z] = jnp.full(labs.shape[1:], -1, jnp.int32)
    labs[z, 0:1, 0:rows] = labels_ref[...]
    for a in range(nsamp):
        first = me * (BLOCKS_DEV * nblk) + sampled_ref[0, a] * nblk
        idents[mine, a] = jnp.full((1, lanes), first, jnp.int32)

    pl.semaphore_wait(barrier, Z - 1 + Q - 1 + sections - 1)

    def half(a):
        return pl.ds(a * per_slot, per_slot)

    def rx_copy(d, a):
        xx = lax.rem(x + d, X)
        return remote(
            centers_hbm.at[half(a)], raw.at[mine, half(a)],
            rx_send_sem.at[d, a], r_recv_sem.at[mine, a], in_row(xx * C + c),
        )

    def rc_own(d, a):
        cc = lax.rem(c + d, C)
        return remote(
            centers_hbm.at[half(a)], raw.at[mine, half(a)],
            rc_send_sem.at[x, d, a], r_recv_sem.at[mine, a], in_row(x * C + cc),
        )

    def rc_forward(xx, d, a):
        cc = lax.rem(c + d, C)
        q = xx * C + c
        return remote(
            raw.at[q, half(a)], raw.at[q, half(a)],
            rc_send_sem.at[xx, d, a], r_recv_sem.at[q, a], in_row(x * C + cc),
        )

    def r_arrived(q, a):
        remote(
            raw.at[q, half(a)], raw.at[q, half(a)],
            rc_send_sem.at[0, 0, a], r_recv_sem.at[q, a], in_row(mine),
        ).wait_recv()

    def id_copy(src, q, index):
        return remote(
            idents.at[src], idents.at[src], id_send_sem.at[index], id_recv_sem.at[src], in_row(q)
        )

    def lab_copy(src, zz, index):
        return remote(
            labs.at[src], labs.at[src], lab_send_sem.at[index], lab_recv_sem.at[src], at_z(zz)
        )

    for a in range(nsamp):
        for d in range(1, X):
            rx_copy(d, a).start()
    for a in range(nsamp):
        for d in range(1, C):
            rc_own(d, a).start()
    for d in range(1, Q):
        id_copy(mine, lax.rem(mine + d, Q), d).start()
    for d in range(1, Z):
        lab_copy(z, lax.rem(z + d, Z), d).start()

    step = 64

    def prepare(q):
        @pl.loop(0, raw.shape[1] // step)
        def _(i):
            at = pl.ds(pl.multiple_of(i * step, step), step)
            valf = raw[q, at, :].astype(jnp.float32)
            inv = lax.rsqrt(jnp.sum(valf * valf, axis=-1, keepdims=True) + 1e-06)
            unit[q, at, :] = (valf * inv).astype(jnp.bfloat16)

    def prepare_chip():
        centers_copy.wait()
        prepare(mine)
        for d in range(1, C):
            q = x * C + lax.rem(c + d, C)
            for a in range(nsamp):
                r_arrived(q, a)
            prepare(q)

    @pl.when(s > 0)
    def _():
        prepare_chip()

    weight_copy.wait()

    @pl.when(s == 0)
    def _():
        in_copy.wait()

    @pl.when(s == sections - 1)
    def _():
        neck_copy.wait()

    def hid_copy(j):
        return remote(
            hid_out.at[j], trunk.at[j], hid_send_sem.at[j], hid_recv_sem.at[j],
            (lax.rem(s + 1, sections), me),
        )

    def emb_copy(j):
        return remote(emb_send.at[j], emb, emb_send_sem.at[j], emb_recv_sem, (j, me))

    for j in range(sections):
        @pl.when(s > 0)
        def _():
            hid_copy(j).wait_recv()

        valf = trunk[j].astype(jnp.float32)
        normed = (layer_norm(valf) * gain_ref[...]).astype(jnp.bfloat16)
        mixed = jnp.dot(normed, weight[...], preferred_element_type=jnp.float32)
        act = mixed * (lax.erf(mixed * (1.0 / math.sqrt(2.0))) + 1.0) * 0.5
        hid_out[j] = (valf + act).astype(jnp.bfloat16)

        @pl.when(s < sections - 1)
        def _():
            if j:
                hid_copy(j - 1).wait_send()
            hid_copy(j).start()

        @pl.when(s == sections - 1)
        def _():
            neck_in = layer_norm(hid_out[j].astype(jnp.float32)).astype(jnp.bfloat16)
            embed = jnp.dot(neck_in, neck[...], preferred_element_type=jnp.float32)
            if j == sections - 1:
                emb[...] = embed.astype(jnp.bfloat16)
            else:
                emb_send[j] = embed.astype(jnp.bfloat16)
                emb_copy(j).start()

    @pl.when(s == 0)
    def _():
        prepare_chip()

    @pl.when(s < sections - 1)
    def _():
        emb_copy(0).wait_recv()

    valf = emb[...].astype(jnp.float32)
    inverse = lax.rsqrt(jnp.sum(valf * valf, axis=-1, keepdims=True) + 1e-06)
    feats[z, 0:rows, :] = (valf * inverse).astype(jnp.bfloat16)

    def f_copy(src, zz, send_sem):
        part = feats.at[src, pl.ds(0, rows)]
        return remote(part, part, send_sem, f_recv_sem.at[src], at_z(zz))

    def fh_copy(d):
        return f_copy(z, lax.rem(h + d, H) * W + w, fh_send_sem.at[d])

    def fw_copy(i, d):
        hh = lax.rem(h + i, H)
        return f_copy(hh * W + w, h * W + lax.rem(w + d, W), fw_send_sem.at[i, d])

    def f_arrived(zz):
        f_copy(zz, zz, fh_send_sem.at[0]).wait_recv()

    for d in range(1, H):
        fh_copy(d).start()
    for d in range(1, W):
        fw_copy(0, d).start()

    tile = 32
    row_index = lax.broadcasted_iota(jnp.int32, (tile, lanes), 0)
    cos_m, sin_m = math.cos(margin_angle), math.sin(margin_angle)

    def scores(zz, base, first_part):
        lab = jnp.broadcast_to(labs[zz, 0:1, :], (tile, lanes)) - row_index

        def shard(q, total):
            for a in range(nsamp):
                cosine = lax.dot_general(
                    unit[q, half(a), :], feats[zz],
                    (((1,), (1,)), ((), ())), preferred_element_type=jnp.float32,
                )
                hit = lab - jnp.broadcast_to(idents[q, a], (tile, lanes))
                for r in range(0, nblk, tile):
                    exps = [
                        jnp.exp(cosine[k * nblk + r:k * nblk + r + tile] * (1.0 / pool_temp))
                        for k in range(nsub)
                    ]
                    summed = exps[0]
                    for k in range(1, nsub):
                        summed = summed + exps[k]
                    pooled = pool_temp * jnp.log(summed * (1.0 / nsub))
                    target = hit == r
                    gap = sine_offset - pooled * pooled
                    rroot = lax.rsqrt(gap)
                    logits = logit_scale * jnp.where(
                        target, pooled * cos_m - gap * rroot * sin_m, pooled
                    )
                    slope = jnp.where(target, cos_m + pooled * sin_m * rroot, 1.0)
                    el = jnp.exp(logits)
                    total = total + el
                    scaled = logit_scale * slope / summed
                    at = slice(r, r + tile)
                    coef_a[zz, q, a, at, :] = el * scaled
                    coef_b[zz, q, a, at, :] = jnp.where(target, scaled, 0.0)
                    for k in range(nsub):
                        expo[zz, q, a, k, at, :] = exps[k].astype(expo.dtype)
            return total

        total = lax.fori_loop(
            base, base + C, shard, jnp.zeros((tile, lanes), jnp.float32)
        )
        total = jnp.sum(total, axis=0, keepdims=True)
        tparts[z, zz] = total if first_part else tparts[z, zz] + total

    for d in range(1, Q):
        q = lax.rem(mine + d, Q)
        id_copy(q, q, 0).wait_recv()
    for d in range(1, Z):
        zz = lax.rem(z + d, Z)
        lab_copy(zz, zz, 0).wait_recv()

    chip = x * C
    scores(z, chip, True)
    for d in range(1, W):
        zz = h * W + lax.rem(w + d, W)
        f_arrived(zz)
        scores(zz, chip, True)
    for i in range(1, H):
        zz = lax.rem(h + i, H) * W + w
        f_arrived(zz)
        for d in range(1, W):
            fw_copy(i, d).start()
        scores(zz, chip, True)

    for d in range(1, X):
        xx = lax.rem(x + d, X)
        for a in range(nsamp):
            r_arrived(xx * C + c, a)
            for e in range(1, C):
                rc_forward(xx, e, a).start()
    for i in range(1, H):
        for d in range(1, W):
            zz = lax.rem(h + i, H) * W + lax.rem(w + d, W)
            f_arrived(zz)
            scores(zz, chip, True)
    for d in range(1, X):
        xx = lax.rem(x + d, X)
        prepare(xx * C + c)
        for e in range(1, C):
            q = xx * C + lax.rem(c + e, C)
            for a in range(nsamp):
                r_arrived(q, a)
            prepare(q)

    @pl.loop(0, Z)
    def _(zz):
        for d in range(1, X):
            scores(zz, lax.rem(x + d, X) * C, False)

    def t_copy(src, zz, index):
        return remote(
            tparts.at[src], tparts.at[src], t_send_sem.at[index], t_recv_sem.at[src], at_z(zz)
        )

    for d in range(1, Z):
        t_copy(z, lax.rem(z + d, Z), d).start()
    for d in range(1, Z):
        zz = lax.rem(z + d, Z)
        t_copy(zz, zz, 0).wait_recv()

    tsum[...] = 1.0 / jnp.sum(tparts[...], axis=0)

    def backward(zz):
        inv_total = jnp.broadcast_to(tsum[zz], (tile, lanes))

        @pl.loop(0, Q)
        def _(q):
            for a in range(nsamp):
                for r in range(0, nblk, tile):
                    at = slice(r, r + tile)
                    factor = coef_a[zz, q, a, at, :] * inv_total - coef_b[zz, q, a, at, :]
                    for k in range(nsub):
                        first = (a * nsub + k) * nblk + r
                        pulled[q, first:first + tile, :] = (
                            factor * expo[zz, q, a, k, at, :].astype(jnp.float32)
                        ).astype(jnp.bfloat16)

        grad = lax.dot_general(
            pulled[...].reshape(-1, lanes), unit[...].reshape(-1, width),
            (((0,), (0,)), ((), ())), preferred_element_type=jnp.float32,
        )
        return grad[0:rows]

    def gw_copy(hh, ww):
        return remote(
            send_w.at[hh * W + ww], recv_w.at[w, hh],
            gw_send_sem.at[hh * W + ww], gw_recv_sem.at[w, hh], at_z(h * W + ww),
        )

    def gh_copy(hh):
        return remote(
            send_h.at[hh], recv_h.at[h], gh_send_sem.at[hh], gh_recv_sem.at[h], at_z(hh * W + w)
        )

    def summed_over_w(hh):
        value = backward(hh * W + w)
        for d in range(1, W):
            ww = lax.rem(w + d, W)
            remote(
                send_w.at[0], recv_w.at[ww, hh],
                gw_send_sem.at[0], gw_recv_sem.at[ww, hh], at_z(z),
            ).wait_recv()
            value = value + recv_w[ww, hh].astype(jnp.float32)
        return value

    far = [lax.rem(h + i, H) for i in range(1, H)]
    for hh in far + [h]:
        for d in range(1, W):
            ww = lax.rem(w + d, W)
            send_w[hh * W + ww] = backward(hh * W + ww).astype(jnp.bfloat16)
            gw_copy(hh, ww).start()
    for hh in far:
        send_h[hh] = summed_over_w(hh).astype(jnp.bfloat16)
        gh_copy(hh).start()
    own_grad = summed_over_w(h)
    for hh in far:
        remote(
            send_h.at[0], recv_h.at[hh], gh_send_sem.at[0], gh_recv_sem.at[hh], at_z(z)
        ).wait_recv()
        own_grad = own_grad + recv_h[hh].astype(jnp.float32)

    valf = emb[...].astype(jnp.float32)
    inverse = lax.rsqrt(jnp.sum(valf * valf, axis=-1, keepdims=True) + 1e-06)
    direction = valf * inverse
    along = jnp.sum(own_grad * direction, axis=-1, keepdims=True)
    out_ref[0] = inverse * (own_grad - along * direction)

    for j in range(sections):
        @pl.when(s < sections - 1)
        def _():
            if j == sections - 1:
                hid_copy(j).wait_send()

        if j < sections - 1:
            @pl.when(s == sections - 1)
            def _():
                emb_copy(j).wait_send()

    for d in range(1, Q):
        id_copy(mine, lax.rem(mine + d, Q), d).wait_send()
    for d in range(1, Z):
        lab_copy(z, lax.rem(z + d, Z), d).wait_send()
    for a in range(nsamp):
        for d in range(1, X):
            rx_copy(d, a).wait_send()
            for e in range(1, C):
                rc_forward(lax.rem(x + d, X), e, a).wait_send()
        for d in range(1, C):
            rc_own(d, a).wait_send()
    for d in range(1, Z):
        t_copy(z, lax.rem(z + d, Z), d).wait_send()
    for d in range(1, H):
        fh_copy(d).wait_send()
        gh_copy(lax.rem(h + d, H)).wait_send()
    for i in range(H):
        for d in range(1, W):
            fw_copy(i, d).wait_send()
            gw_copy(lax.rem(h + i, H), lax.rem(w + d, W)).wait_send()


def shards(H, X, W, C, inputs, section_weight, section_gain, neck_weight, centers, sampled, labels):
    sections = lax.axis_size("section")
    Q, Z = X * C, H * W
    dim = inputs.shape[-1]
    rows = inputs.shape[1] // sections
    _, nsamp, nsub, nblk, width = centers.shape
    lanes = -(-rows // 128) * 128
    bf16, f32 = jnp.bfloat16, jnp.float32
    expo_type = f32 if Z * lanes * Q * nsamp * nsub * nblk * 4 <= 8 * 2**20 else bf16
    dma = pltpu.SemaphoreType.DMA
    vmem = pltpu.VMEM
    flat = centers.reshape(-1, width)
    scratch = [
        vmem((sections, rows, dim), bf16),
        vmem(section_weight.shape[1:], bf16),
        vmem(neck_weight.shape, bf16),
        vmem((Q,) + flat.shape, bf16),
        vmem((Q,) + flat.shape, bf16),
        vmem((sections, rows, dim), bf16),
        vmem((sections, rows, width), bf16),
        vmem((rows, width), bf16),
        vmem((Z, lanes, width), bf16),
        vmem((Z, 8, lanes), jnp.int32),
        vmem((Q, nsamp, 1, lanes), jnp.int32),
        vmem((Z, Q, nsamp, nsub, nblk, lanes), expo_type),
        vmem((Z, Q, nsamp, nblk, lanes), f32),
        vmem((Z, Q, nsamp, nblk, lanes), f32),
        vmem((Z, Z, 1, lanes), f32),
        vmem((Z, 1, lanes), f32),
        vmem((Q, nsamp * nsub * nblk, lanes), bf16),
        vmem((Z, rows, width), bf16),
        vmem((W, H, rows, width), bf16),
        vmem((H, rows, width), bf16),
        vmem((H, rows, width), bf16),
        dma((4,)), dma((sections,)), dma((sections,)), dma((sections,)), dma,
        dma((Q,)), dma((Q,)), dma((Z,)), dma((Z,)), dma((Z,)), dma((Z,)),
        dma((X, nsamp)), dma((X, C, nsamp)), dma((Q, nsamp)),
        dma((H,)), dma((H, W)), dma((Z,)), dma((Z,)), dma((W, H)), dma((H,)), dma((H,)),
    ]
    any_spec = pl.BlockSpec(memory_space=pl.ANY)
    vmem_spec = pl.BlockSpec(memory_space=pltpu.VMEM)
    smem_spec = pl.BlockSpec(memory_space=pltpu.SMEM)
    return pl.pallas_call(
        functools.partial(kernel, sections, H, X, W, C),
        out_shape=jax.ShapeDtypeStruct((1, rows, width), f32),
        in_specs=[any_spec, any_spec, vmem_spec, any_spec, any_spec, smem_spec, vmem_spec],
        out_specs=vmem_spec,
        scratch_shapes=scratch,
        compiler_params=pltpu.CompilerParams(
            collective_id=0, has_side_effects=True, vmem_limit_bytes=62 * 2**20
        ),
        name="arcface_head",
    )(
        inputs.reshape(sections, rows, dim), section_weight[0], section_gain, neck_weight,
        flat, sampled, labels,
    )


def solution(mesh):
    depth, W, C = split_of(mesh.shape["ident"])
    X = 2 if depth % 2 == 0 else 1
    H = depth // X
    in_specs = (
        P("ident", None, None),
        P("section", None, None),
        P("section", None),
        P(),
        P("ident", None, None, None, None),
        P("ident", None),
        P("ident", "section"),
    )
    out_specs = P("ident", "section", None)
    return jax.shard_map(
        functools.partial(shards, H, X, W, C),
        mesh=mesh, in_specs=in_specs, out_specs=out_specs, check_vma=False,
    )
```
